1024 devices in a mesh: fsdp: 128 (over x, z), rep: 8 (over y, core).
Axes of the slice: x: 4, y: 4, z: 32, core: 2. Of those that a mesh axis runs over, the one named last changes fastest.
Arguments:
- grads: bfloat16 [8, 128, 512, 512], P('rep', None, 'fsdp'), may hold values from -0.099609375 to 0.099609375
- owner: int32 [128], replicated, may hold values from 0 to 127, as said below
- left_stat: float32 [128, 2, 512, 512], P('fsdp', None, 'rep'), may hold values from -0.1 to 2.1, as said below
- right_stat: float32 [128, 2, 512, 512], P('fsdp', None, 'rep'), may hold values from -0.1 to 2.1, as said below
- left_root: bfloat16 [128, 2, 512, 512], P('fsdp', None, 'rep'), as said below
- right_root: bfloat16 [128, 2, 512, 512], P('fsdp', None, 'rep'), as said below
Outputs:
- left_new: float32 [128, 2, 512, 512], P('fsdp', None, 'rep')
- right_new: float32 [128, 2, 512, 512], P('fsdp', None, 'rep')
- update: bfloat16 [128, 512, 512], P(None, 'fsdp', 'rep')
The draws below stay inside these ranges and needn't reach their ends.
Inputs may be any that keep to these rules, and one draw needn't show every extreme that they name: `owner`: every fsdp rank owns at most 2 blocks, and some rank owns exactly 2; rank 128 - 1 owns at least one block. `left_stat`: each matrix is symmetric. `right_stat`: each matrix is symmetric. `left_root`: each matrix is symmetric. `right_root`: each matrix is symmetric.
All inputs are finite; a program needn't handle non-finite values.
Results may differ from the reference program's by a relative error of at most 0.023.
Values may be sent and summed in bfloat16 or wider, within the bound.
No kernel may reach another device: no remote copies, remote signals or barrier semaphores. Data moves between devices by JAX's collectives and lax.ppermute only.
A program may use at most 32 MiB of HBM per device.

```python
import jax
import jax.numpy as jnp
from jax import lax

BLOCK = 512
GROUP = 128
SLOTS = 2
BLOCKS = 128
N_FSDP = 128
N_REP = 8


def root_matrix(noise_part, diagonal, magnitude):
    symmetric = (noise_part + jnp.swapaxes(noise_part, -1, -2)) * (0.3 / (2.0 * BLOCK) ** 0.5)
    counter = jnp.arange(BLOCK, dtype=jnp.int32)
    identity = (counter[:, None] == counter[None, :]).astype(jnp.float32)
    return (magnitude * (symmetric + identity * diagonal[..., None])).astype(jnp.bfloat16)


def stat_matrix(noise_part, diagonal):
    symmetric = (noise_part + jnp.swapaxes(noise_part, -1, -2)) * 0.05
    counter = jnp.arange(BLOCK, dtype=jnp.int32)
    identity = (counter[:, None] == counter[None, :]).astype(jnp.float32)
    return (symmetric + identity * diagonal[..., None]).astype(jnp.float32)


def stat_draw(key):
    key_one, key_two = jax.random.split(key)
    full_shape = (N_FSDP, SLOTS, BLOCK, BLOCK)
    noise_part = jnp.clip(0.577 * jax.random.normal(key_one, full_shape, jnp.float32), -1.0, 1.0)
    diagonal = jax.random.uniform(key_two, full_shape[:-1], jnp.float32, 0.5, 1.5)
    return stat_matrix(noise_part, diagonal)


def draw_owner(key, part):
    key = jax.random.fold_in(key, 5)
    key_one, key_two, key_three = jax.random.split(key, 3)
    doubled = jax.random.randint(key_one, (), 1, BLOCKS // SLOTS + 1)
    rank_order = jax.random.permutation(key_two, N_FSDP).astype(jnp.int32)
    counter = jnp.arange(BLOCKS, dtype=jnp.int32)
    position = jnp.where(counter < SLOTS * doubled, counter // SLOTS, counter - (SLOTS - 1) * doubled)
    ordered = rank_order[position]
    ordered = ordered + (N_FSDP - 1 - jnp.max(ordered))
    shuffle = jax.random.permutation(key_three, BLOCKS)
    return ordered[shuffle].astype(jnp.int32)


def draw_left_stat(key, part):
    key = jax.random.fold_in(key, 31)
    return stat_draw(key)


def draw_right_stat(key, part):
    key = jax.random.fold_in(key, 37)
    return stat_draw(key)


def draw_left_root(key, part):
    key = jax.random.fold_in(key, 11)
    key_one, key_two = jax.random.split(key)
    full_shape = (N_FSDP, SLOTS, BLOCK, BLOCK)
    noise_part = jax.random.normal(key_one, full_shape, jnp.float32)
    diagonal = jax.random.uniform(key_two, full_shape[:-1], jnp.float32, 0.8, 1.2)
    return root_matrix(noise_part, diagonal, 4.75)


def draw_right_root(key, part):
    key = jax.random.fold_in(key, 23)
    key_one, key_two = jax.random.split(key)
    full_shape = (N_FSDP, SLOTS, BLOCK, BLOCK)
    noise_part = jax.random.normal(key_one, full_shape, jnp.float32)
    diagonal = jax.random.uniform(key_two, full_shape[:-1], jnp.float32, 0.8, 1.2)
    return root_matrix(noise_part, diagonal, 4.75)


def spiked(result, own_key, source, target, parts, factor):
    owner, partner = [(jnp.arange(result.shape[dim]) // (result.shape[dim] // parts)).reshape([-1 if axis == dim else 1 for axis in range(result.ndim)]) for dim in (source, target)]
    chosen = jax.random.permutation(own_key, parts)[partner]
    strong = (owner == chosen) | (owner == (partner + parts // 2) % parts)
    return jnp.where(strong, factor * result, result)


def block_scale(rng, shape, cuts, least, largest):
    loudness = 1.0
    for dim, blocks in cuts:
        heights = jax.random.uniform(jax.random.fold_in(jax.random.fold_in(rng, 6), dim), (blocks,), jnp.float32, least / len(cuts), largest / len(cuts))
        loudness = loudness * jnp.repeat(jnp.exp(heights), shape[dim] // blocks).reshape((-1,) + (1,) * (len(shape) - 1 - dim))
    return loudness


def bell_draw_with(key, dims, spread, limit, cuts, heavy, kind=jnp.bfloat16):
    values = spread * jax.random.normal(key, dims, jnp.float32)
    if cuts:
        values = values * block_scale(key, dims, cuts, -0.22, 0.18)
    return jnp.clip(spiked(values, jax.random.fold_in(key, 3), *heavy), -limit, limit).astype(kind)


def setup_inputs(seed: int = 0) -> dict:
    splits = jax.random.split(jax.random.key(seed), 7)
    grads = bell_draw_with(splits[0], (N_REP, BLOCKS, BLOCK, BLOCK), 0.0156, 0.099609375, ((0, 8), (2, 128)), (0, 3, 8, 2.0))
    owner = draw_owner(jax.random.fold_in(splits[6], 71), 0)
    left_stat = draw_left_stat(jax.random.fold_in(splits[6], 71), 0)
    right_stat = draw_right_stat(jax.random.fold_in(splits[6], 71), 0)
    left_root = draw_left_root(jax.random.fold_in(splits[6], 71), 0)
    right_root = draw_right_root(jax.random.fold_in(splits[6], 71), 0)
    return {"grads": grads, "owner": owner, "left_stat": left_stat, "right_stat": right_stat, "left_root": left_root, "right_root": right_root}


stat_decay = 0.95


def hadamard(length):
    counter = jnp.arange(length, dtype=jnp.int32)
    correlation = counter[:, None] & counter[None, :]
    parity = jnp.zeros((length, length), jnp.int32)
    for bit_pos in range(length.bit_length() - 1):
        parity = parity ^ ((correlation >> bit_pos) & 1)
    return (1 - 2 * parity).astype(jnp.bfloat16)


def block_gradient(partials, signs):
    shaped = partials.astype(jnp.float32).reshape(N_REP, BLOCK, BLOCK // GROUP, GROUP)
    turned = jnp.einsum("rigk,kj->rigj", shaped, signs.astype(jnp.float32)) * (GROUP ** -0.5)
    peak_abs = jnp.max(jnp.abs(turned), axis=-1, keepdims=True) + 1e-6
    scales = lax.optimization_barrier(peak_abs.astype(jnp.bfloat16)).astype(jnp.float32)
    quantized = (turned / scales).astype(jnp.bfloat16)
    summed = jnp.sum(quantized.astype(jnp.float32) * scales, axis=0).astype(jnp.bfloat16)
    restored = jnp.einsum("igk,kj->igj", summed.astype(jnp.float32), signs.astype(jnp.float32)) * (GROUP ** -0.5)
    return restored.reshape(BLOCK, BLOCK).astype(jnp.bfloat16)


def reference(grads, owner, left_stat, right_stat, left_root, right_root):
    signs = hadamard(GROUP)
    grad_blocks = lax.map(lambda partials: block_gradient(partials, signs), jnp.swapaxes(grads, 0, 1))
    counter = jnp.arange(BLOCKS, dtype=jnp.int32)
    same_owner = owner[:, None] == owner[None, :]
    slot_of = jnp.sum(same_owner & (counter[None, :] < counter[:, None]), axis=1).astype(jnp.int32)

    def per_owner(inputs):
        owner_rank, lstat, rstat, lroot, rroot = inputs
        left_list, right_list, direction_list = [], [], []
        for slot_id in range(SLOTS):
            matches = (owner == owner_rank) & (slot_of == slot_id)
            block_index = jnp.sum(jnp.where(matches, counter, 0)).astype(jnp.int32)
            gradient = jnp.where(jnp.any(matches), grad_blocks[block_index], jnp.zeros((BLOCK, BLOCK), grad_blocks.dtype))
            left_list.append(stat_decay * lstat[slot_id] + (1 - stat_decay) * jnp.dot(gradient, gradient.T, preferred_element_type=jnp.float32))
            right_list.append(stat_decay * rstat[slot_id] + (1 - stat_decay) * jnp.dot(gradient.T, gradient, preferred_element_type=jnp.float32))
            middle = jnp.dot(gradient, rroot[slot_id], preferred_element_type=jnp.float32).astype(jnp.bfloat16)
            direction_list.append(jnp.dot(lroot[slot_id], middle, preferred_element_type=jnp.float32).astype(jnp.bfloat16))
        return jnp.stack(left_list), jnp.stack(right_list), jnp.stack(direction_list)

    left_new, right_new, directions = lax.map(per_owner, (jnp.arange(N_FSDP, dtype=jnp.int32), left_stat, right_stat, left_root, right_root))
    update = directions[owner, slot_of]
    return left_new, right_new, update
```

```python
import jax
import jax.numpy as jnp
from jax import lax
from jax.sharding import PartitionSpec as P

GROUP = 128
SLOTS = 2
DECAY = 0.95


def hadamard(length):
    counter = jnp.arange(length, dtype=jnp.int32)
    correlation = counter[:, None] & counter[None, :]
    parity = jnp.zeros((length, length), jnp.int32)
    for bit_pos in range(length.bit_length() - 1):
        parity = parity ^ correlation >> bit_pos & 1
    return (1 - 2 * parity).astype(jnp.bfloat16)


def mm(a, b):
    return jnp.dot(a, b, preferred_element_type=jnp.float32)


def on_device(grads, owner, left_stat, right_stat, left_root, right_root):
    bf, f32, i32 = jnp.bfloat16, jnp.float32, jnp.int32
    signs = hadamard(GROUP)
    norm = GROUP ** (-0.5)
    x = grads[0]
    nb, rows, width = x.shape
    nf = lax.axis_size("fsdp")
    nrep = lax.axis_size("rep")
    groups = width // GROUP
    halves = nrep // groups
    per = rows // halves
    slab = width // nrep

    lroot = lax.all_gather(left_root[0], "rep", axis=1, tiled=True)

    turned = jnp.einsum("brgk,kj->brgj", x.reshape(nb, rows, groups, GROUP), signs,
                        preferred_element_type=f32) * norm
    peak = jnp.max(jnp.abs(turned), axis=-1) + 1e-06
    scales = lax.optimization_barrier(peak.astype(bf)).astype(f32)
    codes = (turned / scales[..., None]).astype(bf)
    terms = (codes.astype(f32) * scales[..., None]).astype(bf)
    send = terms.reshape(nb, halves, per, groups, GROUP).transpose(3, 1, 0, 2, 4)
    send = send.reshape(nrep, nb * per, GROUP)
    got = lax.all_to_all(send, "rep", split_axis=0, concat_axis=0, tiled=True)
    summed = jnp.sum(got.astype(f32), axis=0).astype(bf)

    counter = jnp.arange(nb, dtype=i32)
    same = owner[:, None] == owner[None, :]
    slot_of = jnp.sum(same & (counter[None, :] < counter[:, None]), axis=1)
    place = owner * SLOTS + slot_of
    out_row = jnp.arange(nf * SLOTS * per, dtype=i32)
    in_row = jnp.arange(nb * per, dtype=i32)
    key_in = jnp.repeat(place, per) * per + in_row % per
    route = (out_row[:, None] == key_in[None, :]).astype(bf)
    outgoing = mm(route, summed).astype(bf).reshape(nf, SLOTS * per, GROUP)
    arrived = lax.all_to_all(outgoing, "fsdp", split_axis=0, concat_axis=0, tiled=True)

    copies = jnp.broadcast_to(arrived.reshape(1, nf * SLOTS * per, GROUP), (nrep, nf * SLOTS * per, GROUP))
    whole = lax.all_to_all(copies, "rep", split_axis=0, concat_axis=0, tiled=True)
    whole = whole.reshape(groups, halves, nf, SLOTS, per, GROUP).transpose(3, 2, 1, 4, 0, 5)
    restored = jnp.einsum("sigk,kj->sigj", whole.reshape(SLOTS, width, groups, GROUP), signs,
                          preferred_element_type=f32) * norm
    gradient = restored.reshape(SLOTS, width, width).astype(bf)

    rank = lax.axis_index("rep")
    own_rows = lax.dynamic_slice_in_dim(gradient, rank * slab, slab, axis=1)
    own_cols = lax.dynamic_slice_in_dim(gradient, rank * slab, slab, axis=2)
    middle = jnp.einsum("sik,sck->sic", gradient, right_root[0], preferred_element_type=f32).astype(bf)
    direction = jnp.einsum("sik,skc->isc", lroot, middle, preferred_element_type=f32).astype(bf)
    packed = direction.reshape(nf, rows, SLOTS * slab)
    back = lax.all_to_all(packed, "fsdp", split_axis=0, concat_axis=0, tiled=True)

    left_gram = jnp.einsum("sik,sjk->sij", own_rows, gradient, preferred_element_type=f32)
    right_gram = jnp.einsum("ski,skj->sij", own_cols, gradient, preferred_element_type=f32)
    left_new = DECAY * left_stat[0] + (1 - DECAY) * left_gram
    right_new = DECAY * right_stat[0] + (1 - DECAY) * right_gram

    pick = (place[:, None] == jnp.arange(nf * SLOTS, dtype=i32)[None, :]).astype(bf).reshape(nb, nf, SLOTS)
    update = jnp.einsum("bfs,frsc->brc", pick, back.reshape(nf, rows, SLOTS, slab),
                        preferred_element_type=f32).astype(bf)
    return (left_new[None], right_new[None], update)


def solution(mesh):
    in_specs = (
        P("rep", None, "fsdp", None),
        P(),
        P("fsdp", None, "rep", None),
        P("fsdp", None, "rep", None),
        P("fsdp", None, "rep", None),
        P("fsdp", None, "rep", None),
    )
    out_specs = (P("fsdp", None, "rep", None), P("fsdp", None, "rep", None), P(None, "fsdp", "rep"))
    return jax.shard_map(on_device, mesh=mesh, in_specs=in_specs, out_specs=out_specs, check_vma=False)
```

```python
import jax
import jax.numpy as jnp
from jax import lax
from jax.sharding import PartitionSpec as P

GROUP = 128
SLOTS = 2
DECAY = 0.95


def hadamard(length):
    counter = jnp.arange(length, dtype=jnp.int32)
    correlation = counter[:, None] & counter[None, :]
    parity = jnp.zeros((length, length), jnp.int32)
    for bit_pos in range(length.bit_length() - 1):
        parity = parity ^ correlation >> bit_pos & 1
    return (1 - 2 * parity).astype(jnp.bfloat16)


def mm(a, b):
    return jnp.dot(a, b, preferred_element_type=jnp.float32)


def on_device(grads, owner, left_stat, right_stat, left_root, right_root):
    bf, f32, i32 = jnp.bfloat16, jnp.float32, jnp.int32
    signs = hadamard(GROUP)
    norm = GROUP ** (-0.5)
    x = grads[0]
    nb, rows, width = x.shape
    nf = lax.axis_size("fsdp")
    nrep = lax.axis_size("rep")
    groups = width // GROUP
    halves = nrep // groups
    per = rows // halves
    slab = width // nrep

    turned = jnp.einsum("brgk,kj->brgj", x.reshape(nb, rows, groups, GROUP), signs,
                        preferred_element_type=f32) * norm
    peak = jnp.max(jnp.abs(turned), axis=-1) + 1e-06
    scales = lax.optimization_barrier(peak.astype(bf)).astype(f32)
    codes = (turned / scales[..., None]).astype(bf)
    terms = (codes.astype(f32) * scales[..., None]).astype(bf)
    send = terms.reshape(nb, halves, per, groups, GROUP).transpose(3, 1, 0, 2, 4)
    send = send.reshape(nrep, nb * per, GROUP)
    got = lax.all_to_all(send, "rep", split_axis=0, concat_axis=0, tiled=True)
    summed = jnp.sum(got.astype(f32), axis=0).astype(bf)

    counter = jnp.arange(nb, dtype=i32)
    same = owner[:, None] == owner[None, :]
    slot_of = jnp.sum(same & (counter[None, :] < counter[:, None]), axis=1)
    place = owner * SLOTS + slot_of
    out_row = jnp.arange(nf * SLOTS * per, dtype=i32)
    in_row = jnp.arange(nb * per, dtype=i32)
    key_in = jnp.repeat(place, per) * per + in_row % per
    route = (out_row[:, None] == key_in[None, :]).astype(bf)
    outgoing = mm(route, summed).astype(bf).reshape(nf, SLOTS * per, GROUP)
    outgoing, lroot_rows = lax.optimization_barrier((outgoing, left_root[0]))
    lroot_flat = lroot_rows.reshape(1, SLOTS * slab * groups, GROUP)
    lroot_copies = jnp.broadcast_to(lroot_flat, (nrep, SLOTS * slab * groups, GROUP))
    arrived = lax.all_to_all(outgoing, "fsdp", split_axis=0, concat_axis=0, tiled=True)
    lroot = lax.all_to_all(lroot_copies, "rep", split_axis=0, concat_axis=0, tiled=True)
    lroot = lroot.reshape(nrep, SLOTS, slab, width).transpose(1, 0, 2, 3).reshape(SLOTS, width, width)

    chip_mates = [[h + halves * g for g in range(groups)] for h in range(halves)]
    copies = jnp.broadcast_to(arrived.reshape(1, nf * SLOTS * per, GROUP), (groups, nf * SLOTS * per, GROUP))
    mine = lax.all_to_all(copies, "rep", split_axis=0, concat_axis=0, axis_index_groups=chip_mates, tiled=True)
    other = lax.ppermute(mine, "rep", [(j, j + 1 - 2 * (j % 2)) for j in range(nrep)])
    rank = lax.axis_index("rep")
    first = rank % halves == 0
    whole = jnp.stack([jnp.where(first, mine, other), jnp.where(first, other, mine)], axis=1)
    whole = whole.reshape(groups, halves, nf, SLOTS, per, GROUP).transpose(3, 2, 1, 4, 0, 5)
    restored = jnp.einsum("sigk,kj->sigj", whole.reshape(SLOTS, width, groups, GROUP), signs,
                          preferred_element_type=f32) * norm
    gradient = restored.reshape(SLOTS, width, width).astype(bf)

    own_rows = lax.dynamic_slice_in_dim(gradient, rank * slab, slab, axis=1)
    own_cols = lax.dynamic_slice_in_dim(gradient, rank * slab, slab, axis=2)
    middle = jnp.einsum("sik,sck->sic", gradient, right_root[0], preferred_element_type=f32).astype(bf)
    direction = jnp.einsum("sik,skc->isc", lroot, middle, preferred_element_type=f32).astype(bf)
    packed = direction.reshape(nf, rows, SLOTS * slab)
    back = lax.all_to_all(packed, "fsdp", split_axis=0, concat_axis=0, tiled=True)

    left_gram = jnp.einsum("sik,sjk->sij", own_rows, gradient, preferred_element_type=f32)
    right_gram = jnp.einsum("ski,skj->sij", own_cols, gradient, preferred_element_type=f32)
    left_new = DECAY * left_stat[0] + (1 - DECAY) * left_gram
    right_new = DECAY * right_stat[0] + (1 - DECAY) * right_gram

    pick = (place[:, None] == jnp.arange(nf * SLOTS, dtype=i32)[None, :]).astype(bf).reshape(nb, nf, SLOTS)
    update = jnp.einsum("bfs,frsc->brc", pick, back.reshape(nf, rows, SLOTS, slab),
                        preferred_element_type=f32).astype(bf)
    return (left_new[None], right_new[None], update)


def solution(mesh):
    in_specs = (
        P("rep", None, "fsdp", None),
        P(),
        P("fsdp", None, "rep", None),
        P("fsdp", None, "rep", None),
        P("fsdp", None, "rep", None),
        P("fsdp", None, "rep", None),
    )
    out_specs = (P("fsdp", None, "rep", None), P("fsdp", None, "rep", None), P(None, "fsdp", "rep"))
    return jax.shard_map(on_device, mesh=mesh, in_specs=in_specs, out_specs=out_specs, check_vma=False)
```

```python
import jax
import jax.numpy as jnp
from jax import lax
from jax.experimental import pallas as pl
from jax.experimental.pallas import tpu as pltpu
from jax.sharding import PartitionSpec as P

GROUP = 128
SLOTS = 2
DECAY = 0.95
NORM = GROUP ** (-0.5)
BF, F32, I32 = jnp.bfloat16, jnp.float32, jnp.int32
VMEM_BYTES = 48 * 1024 * 1024


def hadamard():
    i = lax.broadcasted_iota(I32, (GROUP, GROUP), 0)
    j = lax.broadcasted_iota(I32, (GROUP, GROUP), 1)
    bits = i & j
    parity = jnp.zeros((GROUP, GROUP), I32)
    for k in range(GROUP.bit_length() - 1):
        parity = parity ^ ((bits >> k) & 1)
    return (1 - 2 * parity).astype(F32).astype(BF)


def mm(a, b):
    return jnp.dot(a, b, preferred_element_type=F32)


def mm_t(a, b):
    return lax.dot_general(a, b, (((1,), (1,)), ((), ())), preferred_element_type=F32)


def code_kernel(x_ref, out_ref):
    blocks, rows, width = x_ref.shape
    nrep, _, _ = out_ref.shape
    groups = width // GROUP
    halves = nrep // groups
    per = rows // halves
    signs = hadamard()
    step = 256 // rows
    o = lax.broadcasted_iota(I32, (256, 256), 0)
    i = lax.broadcasted_iota(I32, (256, 256), 1)
    perm = ((i // rows == o % step) & (i % rows == o // step)).astype(F32).astype(BF)
    for t in range(blocks // step):
        x = x_ref[t * step:(t + 1) * step].reshape(256, width)
        x = mm(perm, x).astype(BF)
        for g in range(groups):
            turned = mm(x[:, g * GROUP:(g + 1) * GROUP], signs) * NORM
            peak = jnp.max(jnp.abs(turned), axis=1, keepdims=True) + 1e-06
            scale = peak.astype(BF).astype(F32)
            codes = (turned / scale).astype(BF).astype(F32)
            terms = (codes * scale).astype(BF)
            for h in range(halves):
                for r in range(per):
                    row = (h * per + r) * step
                    out_ref[g * halves + h, r * blocks + t * step:r * blocks + (t + 1) * step, :] = (
                        terms[row:row + step])


def root_kernel(rank_ref, mine_ref, other_ref, rroot_ref, *refs):
    *hop_refs, grad_ref, out_ref = refs
    groups, _, _ = mine_ref.shape
    slots, width, _ = grad_ref.shape
    slab = rroot_ref.shape[1]
    rank = rank_ref[0]
    core = rank % 2
    chip = rank // 2
    signs = hadamard()
    o = lax.broadcasted_iota(I32, (256, 256), 0)
    i = lax.broadcasted_iota(I32, (256, 256), 1)
    half = jnp.where(i < 128, core, 1 - core)
    from_row = ((i % 128) // 4) * 4 + half * 2 + i % 2
    perm = ((o % 128 == from_row) & (o // 128 == (i // 2) % 2)).astype(F32).astype(BF)
    for t in range(width // 128):
        rows = slice(t * 128, (t + 1) * 128)
        for g in range(groups):
            both = jnp.concatenate([mine_ref[g, rows, :], other_ref[g, rows, :]], axis=0)
            placed = mm(perm, both).astype(BF)
            block = (mm(placed, signs) * NORM).astype(BF)
            for s in range(slots):
                grad_ref[s, rows, g * GROUP:(g + 1) * GROUP] = block[s * 128:(s + 1) * 128]
    for s in range(slots):
        middle = mm_t(grad_ref[s], rroot_ref[s]).astype(BF)
        for d, hop_ref in enumerate(hop_refs):
            from_chip = (chip + groups - d) % groups
            left = hop_ref[:, s * slab:(s + 1) * slab, :].reshape(2 * slab, width)
            rows = mm(left, middle).astype(BF)
            for k in range(2):
                start = pl.multiple_of((from_chip * 2 + (core + k) % 2) * slab, slab)
                out_ref[pl.ds(start, slab), s * slab:(s + 1) * slab] = rows[k * slab:(k + 1) * slab]


def kernel_params():
    return pltpu.CompilerParams(vmem_limit_bytes=VMEM_BYTES)


def in_vmem():
    return pl.BlockSpec(memory_space=pltpu.VMEM)


def code_call(x, nrep):
    nb, rows, width = x.shape
    per = rows * width // GROUP // nrep
    return pl.pallas_call(
        code_kernel,
        out_shape=jax.ShapeDtypeStruct((nrep, nb * per, GROUP), BF),
        in_specs=[in_vmem()],
        out_specs=in_vmem(),
        compiler_params=kernel_params(),
    )(x)


def root_call(rank, mine, other, hops, rroot):
    slots, slab, width = rroot.shape
    return pl.pallas_call(
        root_kernel,
        out_shape=(jax.ShapeDtypeStruct((slots, width, width), BF),
                   jax.ShapeDtypeStruct((width, slots * slab), BF)),
        in_specs=[pl.BlockSpec(memory_space=pltpu.SMEM)] + [in_vmem()] * (3 + len(hops)),
        out_specs=(in_vmem(), in_vmem()),
        compiler_params=kernel_params(),
    )(rank, mine, other, rroot, *hops)


def on_device(grads, owner, left_stat, right_stat, left_root, right_root):
    x = grads[0]
    nb, rows, width = x.shape
    nf = lax.axis_size("fsdp")
    nrep = lax.axis_size("rep")
    groups = width // GROUP
    halves = nrep // groups
    per = rows // halves
    slab = width // nrep
    part = nf * SLOTS * per
    rank = lax.axis_index("rep")

    got = lax.all_to_all(code_call(x, nrep), "rep", split_axis=0, concat_axis=0, tiled=True)
    summed = jnp.sum(got.astype(F32), axis=0).astype(BF)

    counter = jnp.arange(nb, dtype=I32)
    same = owner[:, None] == owner[None, :]
    slot_of = jnp.sum(same & (counter[None, :] < counter[:, None]), axis=1)
    place = owner * SLOTS + slot_of
    key_in = jnp.concatenate([place * per + r for r in range(per)])
    route = (jnp.arange(part, dtype=I32)[:, None] == key_in[None, :]).astype(BF)
    outgoing = mm(route, summed).astype(BF).reshape(nf, SLOTS * per, GROUP)

    outgoing, lroot_rows = lax.optimization_barrier((outgoing, left_root[0]))
    arrived = lax.all_to_all(outgoing, "fsdp", split_axis=0, concat_axis=0, tiled=True)
    own = lroot_rows.reshape(SLOTS * slab, width)
    swap = [(j, j + 1 - 2 * (j % 2)) for j in range(nrep)]
    pair = jnp.stack([own, lax.ppermute(own, "rep", swap)])
    hops = [pair]
    for d in range(1, groups):
        hops.append(lax.ppermute(pair, "rep", [(j, (j + halves * d) % nrep) for j in range(nrep)]))
    arrived, hops = lax.optimization_barrier((arrived, hops))

    chip_mates = [[h + halves * g for g in range(groups)] for h in range(halves)]
    copies = jnp.broadcast_to(arrived.reshape(1, part, GROUP), (groups, part, GROUP))
    mine = lax.all_to_all(copies, "rep", split_axis=0, concat_axis=0, axis_index_groups=chip_mates, tiled=True)
    other = lax.ppermute(mine, "rep", swap)
    gradient, direction = root_call(rank.reshape(1), mine, other, hops, right_root[0])
    packed = direction.reshape(nf, rows, SLOTS * slab)
    back = lax.all_to_all(packed, "fsdp", split_axis=0, concat_axis=0, tiled=True)

    own_rows = lax.dynamic_slice_in_dim(gradient, rank * slab, slab, axis=1)
    own_cols = lax.dynamic_slice_in_dim(gradient, rank * slab, slab, axis=2)
    left_gram = jnp.einsum("sik,sjk->sij", own_rows, gradient, preferred_element_type=F32)
    right_gram = jnp.einsum("ski,skj->sij", own_cols, gradient, preferred_element_type=F32)
    left_new = DECAY * left_stat[0] + (1 - DECAY) * left_gram
    right_new = DECAY * right_stat[0] + (1 - DECAY) * right_gram

    pick = (place[:, None] == jnp.arange(nf * SLOTS, dtype=I32)[None, :]).astype(BF).reshape(nb, nf, SLOTS)
    update = jnp.einsum("bfs,frsc->brc", pick, back.reshape(nf, rows, SLOTS, slab),
                        preferred_element_type=F32).astype(BF)
    return (left_new[None], right_new[None], update)


def solution(mesh):
    in_specs = (
        P("rep", None, "fsdp", None),
        P(),
        P("fsdp", None, "rep", None),
        P("fsdp", None, "rep", None),
        P("fsdp", None, "rep", None),
        P("fsdp", None, "rep", None),
    )
    out_specs = (P("fsdp", None, "rep", None), P("fsdp", None, "rep", None), P(None, "fsdp", "rep"))
    return jax.shard_map(on_device, mesh=mesh, in_specs=in_specs, out_specs=out_specs, check_vma=False)
```

```python
import jax
import jax.numpy as jnp
from jax import lax
from jax.experimental import pallas as pl
from jax.experimental.pallas import tpu as pltpu
from jax.sharding import PartitionSpec as P

GROUP = 128
SLOTS = 2
DECAY = 0.95
NORM = GROUP ** (-0.5)
BF, F32, I32 = jnp.bfloat16, jnp.float32, jnp.int32
VMEM_BYTES = 48 * 1024 * 1024


def hadamard():
    i = lax.broadcasted_iota(I32, (GROUP, GROUP), 0)
    j = lax.broadcasted_iota(I32, (GROUP, GROUP), 1)
    bits = i & j
    parity = jnp.zeros((GROUP, GROUP), I32)
    for k in range(GROUP.bit_length() - 1):
        parity = parity ^ ((bits >> k) & 1)
    return (1 - 2 * parity).astype(F32).astype(BF)


def mm(a, b):
    return jnp.dot(a, b, preferred_element_type=F32)


def mm_t(a, b):
    return lax.dot_general(a, b, (((1,), (1,)), ((), ())), preferred_element_type=F32)


def code_kernel(x_ref, out_ref):
    blocks, rows, width = x_ref.shape
    nrep, _, _ = out_ref.shape
    groups = width // GROUP
    halves = nrep // groups
    per = rows // halves
    signs = hadamard()
    step = 256 // rows
    o = lax.broadcasted_iota(I32, (256, 256), 0)
    i = lax.broadcasted_iota(I32, (256, 256), 1)
    perm = ((i // rows == o % step) & (i % rows == o // step)).astype(F32).astype(BF)
    for t in range(blocks // step):
        x = x_ref[t * step:(t + 1) * step].reshape(256, width)
        x = mm(perm, x).astype(BF)
        for g in range(groups):
            turned = mm(x[:, g * GROUP:(g + 1) * GROUP], signs) * NORM
            peak = jnp.max(jnp.abs(turned), axis=1, keepdims=True) + 1e-06
            scale = peak.astype(BF).astype(F32)
            codes = (turned / scale).astype(BF).astype(F32)
            terms = (codes * scale).astype(BF)
            for h in range(halves):
                for r in range(per):
                    row = (h * per + r) * step
                    out_ref[g * halves + h, r * blocks + t * step:r * blocks + (t + 1) * step, :] = (
                        terms[row:row + step])


def root_kernel(rank_ref, mine_ref, other_ref, hops_ref, swapped_ref, rroot_ref, grad_ref, out_ref):
    groups, _, _ = mine_ref.shape
    slots, width, _ = grad_ref.shape
    slab = rroot_ref.shape[1]
    rank = rank_ref[0]
    core = rank % 2
    chip = rank // 2
    one = hadamard()
    none = jnp.zeros_like(one)
    signs = jnp.concatenate([jnp.concatenate([one, none], axis=1), jnp.concatenate([none, one], axis=1)], axis=0)
    o = lax.broadcasted_iota(I32, (256, 256), 0)
    i = lax.broadcasted_iota(I32, (256, 256), 1)
    half = jnp.where(i < 128, core, 1 - core)
    from_row = ((i % 128) // 4) * 4 + half * 2 + i % 2
    perm = ((o % 128 == from_row) & (o // 128 == (i // 2) % 2)).astype(F32).astype(BF)
    tiles = width // 128
    placed = []
    for t in range(tiles):
        rows = slice(t * 128, (t + 1) * 128)
        both = jnp.concatenate([
            jnp.concatenate([mine_ref[g, rows, :] for g in range(groups)], axis=1),
            jnp.concatenate([other_ref[g, rows, :] for g in range(groups)], axis=1)], axis=0)
        placed.append(mm(perm, both).astype(BF))
    coded = [jnp.concatenate([p[s * 128:(s + 1) * 128] for p in placed], axis=0) for s in range(slots)]
    middles = []
    for s in range(slots):
        grad = jnp.concatenate(
            [(mm(coded[s][:, c:c + 256], signs) * NORM).astype(BF) for c in range(0, width, 256)], axis=1)
        grad_ref[s] = grad
        middles.append(mm_t(grad, rroot_ref[s]).astype(BF))
    for s in range(slots):
        for k, ref in enumerate((hops_ref, swapped_ref)):
            left = ref[:, s * slab:(s + 1) * slab, :].reshape(groups * slab, width)
            rows = mm(left, middles[s]).astype(BF)
            for d in range(groups):
                start = ((chip + groups - d) % groups * 2 + (core + k) % 2) * slab
                out_ref[pl.ds(pl.multiple_of(start, slab), slab), s * slab:(s + 1) * slab] = (
                    rows[d * slab:(d + 1) * slab])


def kernel_params():
    return pltpu.CompilerParams(vmem_limit_bytes=VMEM_BYTES)


def in_vmem():
    return pl.BlockSpec(memory_space=pltpu.VMEM)


def code_call(x, nrep):
    nb, rows, width = x.shape
    per = rows * width // GROUP // nrep
    return pl.pallas_call(
        code_kernel,
        out_shape=jax.ShapeDtypeStruct((nrep, nb * per, GROUP), BF),
        in_specs=[in_vmem()],
        out_specs=in_vmem(),
        compiler_params=kernel_params(),
    )(x)


def root_call(rank, mine, other, hops, swapped, rroot):
    slots, slab, width = rroot.shape
    return pl.pallas_call(
        root_kernel,
        out_shape=(jax.ShapeDtypeStruct((slots, width, width), BF),
                   jax.ShapeDtypeStruct((width, slots * slab), BF)),
        in_specs=[pl.BlockSpec(memory_space=pltpu.SMEM)] + [in_vmem()] * 5,
        out_specs=(in_vmem(), in_vmem()),
        compiler_params=kernel_params(),
    )(rank, mine, other, hops, swapped, rroot)


def on_device(grads, owner, left_stat, right_stat, left_root, right_root):
    x = grads[0]
    nb, rows, width = x.shape
    nf = lax.axis_size("fsdp")
    nrep = lax.axis_size("rep")
    groups = width // GROUP
    halves = nrep // groups
    per = rows // halves
    slab = width // nrep
    part = nf * SLOTS * per
    rank = lax.axis_index("rep")

    got = lax.all_to_all(code_call(x, nrep), "rep", split_axis=0, concat_axis=0, tiled=True)
    summed = jnp.sum(got.astype(F32), axis=0).astype(BF)

    counter = jnp.arange(nb, dtype=I32)
    same = owner[:, None] == owner[None, :]
    slot_of = jnp.sum(same & (counter[None, :] < counter[:, None]), axis=1)
    place = owner * SLOTS + slot_of
    key_in = jnp.concatenate([place * per + r for r in range(per)])
    route = (jnp.arange(part, dtype=I32)[:, None] == key_in[None, :]).astype(BF)
    outgoing = mm(route, summed).astype(BF).reshape(nf, SLOTS * per, GROUP)

    outgoing, lroot_rows = lax.optimization_barrier((outgoing, left_root[0]))
    arrived = lax.all_to_all(outgoing, "fsdp", split_axis=0, concat_axis=0, tiled=True)
    own = lroot_rows.reshape(SLOTS * slab, width)
    swap = [(j, j + 1 - 2 * (j % 2)) for j in range(nrep)]
    hops = [own]
    for d in range(1, groups):
        hops.append(lax.ppermute(own, "rep", [(j, (j + halves * d) % nrep) for j in range(nrep)]))
    arrived, hops = lax.optimization_barrier((arrived, hops))
    hops = jnp.stack(hops)
    swapped = lax.ppermute(hops, "rep", swap)

    chip_mates = [[h + halves * g for g in range(groups)] for h in range(halves)]
    copies = jnp.broadcast_to(arrived.reshape(1, part, GROUP), (groups, part, GROUP))
    mine = lax.all_to_all(copies, "rep", split_axis=0, concat_axis=0, axis_index_groups=chip_mates, tiled=True)
    other = lax.ppermute(mine, "rep", swap)
    gradient, direction = root_call(rank.reshape(1), mine, other, hops, swapped, right_root[0])
    packed = direction.reshape(nf, rows, SLOTS * slab)
    back = lax.all_to_all(packed, "fsdp", split_axis=0, concat_axis=0, tiled=True)

    own_rows = lax.dynamic_slice_in_dim(gradient, rank * slab, slab, axis=1)
    own_cols = lax.dynamic_slice_in_dim(gradient, rank * slab, slab, axis=2)
    left_gram = jnp.einsum("sik,sjk->sij", own_rows, gradient, preferred_element_type=F32)
    right_gram = jnp.einsum("ski,skj->sij", own_cols, gradient, preferred_element_type=F32)
    left_new = DECAY * left_stat[0] + (1 - DECAY) * left_gram
    right_new = DECAY * right_stat[0] + (1 - DECAY) * right_gram

    pick = (place[:, None] == jnp.arange(nf * SLOTS, dtype=I32)[None, :]).astype(BF).reshape(nb, nf, SLOTS)
    update = jnp.einsum("bfs,frsc->brc", pick, back.reshape(nf, rows, SLOTS, slab),
                        preferred_element_type=F32).astype(BF)
    return (left_new[None], right_new[None], update)


def solution(mesh):
    in_specs = (
        P("rep", None, "fsdp", None),
        P(),
        P("fsdp", None, "rep", None),
        P("fsdp", None, "rep", None),
        P("fsdp", None, "rep", None),
        P("fsdp", None, "rep", None),
    )
    out_specs = (P("fsdp", None, "rep", None), P("fsdp", None, "rep", None), P(None, "fsdp", "rep"))
    return jax.shard_map(on_device, mesh=mesh, in_specs=in_specs, out_specs=out_specs, check_vma=False)
```

```python
import jax
import jax.numpy as jnp
from jax import lax
from jax.experimental import pallas as pl
from jax.experimental.pallas import tpu as pltpu
from jax.sharding import Mesh, PartitionSpec as P

GROUP = 128
SLOTS = 2
FSDP, REP = ("x", "z"), ("y", "core")
DECAY = 0.95
NORM = GROUP ** (-0.5)
BF, F32, I32 = jnp.bfloat16, jnp.float32, jnp.int32
VMEM_BYTES = 24 * 1024 * 1024


def hadamard():
    i = lax.broadcasted_iota(I32, (GROUP, GROUP), 0)
    j = lax.broadcasted_iota(I32, (GROUP, GROUP), 1)
    bits = i & j
    parity = jnp.zeros((GROUP, GROUP), I32)
    for k in range(GROUP.bit_length() - 1):
        parity = parity ^ ((bits >> k) & 1)
    return (1 - 2 * parity).astype(F32).astype(BF)


def mm(a, b):
    return jnp.dot(a, b, preferred_element_type=F32)


def mm_t(a, b):
    return lax.dot_general(a, b, (((1,), (1,)), ((), ())), preferred_element_type=F32)


def code_kernel(x_ref, out_ref):
    blocks, rows, width = x_ref.shape
    nrep, _, _ = out_ref.shape
    groups = width // GROUP
    halves = nrep // groups
    per = rows // halves
    signs = hadamard()
    step = 256 // rows
    o = lax.broadcasted_iota(I32, (256, 256), 0)
    i = lax.broadcasted_iota(I32, (256, 256), 1)
    perm = ((i // rows == o % step) & (i % rows == o // step)).astype(F32).astype(BF)
    for t in range(blocks // step):
        x = x_ref[t * step:(t + 1) * step].reshape(256, width)
        x = mm(perm, x).astype(BF)
        for g in range(groups):
            turned = mm(x[:, g * GROUP:(g + 1) * GROUP], signs) * NORM
            peak = jnp.max(jnp.abs(turned), axis=1, keepdims=True) + 1e-06
            scale = peak.astype(BF).astype(F32)
            codes = (turned / scale).astype(BF).astype(F32)
            terms = (codes * scale).astype(BF)
            for h in range(halves):
                for r in range(per):
                    row = (h * per + r) * step
                    out_ref[g * halves + h, r * blocks + t * step:r * blocks + (t + 1) * step, :] = (
                        terms[row:row + step])


def route_kernel(got_ref, route_ref, out_ref):
    total = got_ref[0].astype(F32)
    for k in range(1, got_ref.shape[0]):
        total += got_ref[k].astype(F32)
    out_ref[...] = mm(route_ref[...], total.astype(BF)).astype(BF)


def pick_kernel(back_ref, pick_ref, out_ref):
    rows, slab, blocks = out_ref.shape
    back = back_ref[...].astype(F32).T.astype(BF)
    total = mm(back[:slab], pick_ref[0]) + mm(back[slab:], pick_ref[1])
    for r in range(rows):
        out_ref[r] = total[:, r * blocks:(r + 1) * blocks].astype(BF)


def root_kernel(rank_ref, mine_ref, other_ref, hops_ref, swapped_ref, rroot_ref, grad_ref, out_ref):
    groups = hops_ref.shape[0]
    slots, width, _ = grad_ref.shape
    slab = rroot_ref.shape[1]
    rank = rank_ref[0]
    core = rank % 2
    chip = rank // 2
    one = hadamard()
    none = jnp.zeros_like(one)
    signs = jnp.concatenate([jnp.concatenate([one, none], axis=1), jnp.concatenate([none, one], axis=1)], axis=0)
    o = lax.broadcasted_iota(I32, (256, 256), 0)
    i = lax.broadcasted_iota(I32, (256, 256), 1)
    half = jnp.where(i < 128, core, 1 - core)
    from_row = ((i % 128) // 4) * 4 + half * 2 + i % 2
    perm = ((o % 128 == from_row) & (o // 128 == (i // 2) % 2)).astype(F32).astype(BF)
    tiles = width // 128
    placed = []
    for t in range(tiles):
        both = jnp.concatenate([
            jnp.concatenate([ref[t * groups + g] for g in range(groups)], axis=1) for ref in (mine_ref, other_ref)], axis=0)
        placed.append(mm(perm, both).astype(BF))
    coded = [jnp.concatenate([p[s * 128:(s + 1) * 128] for p in placed], axis=0) for s in range(slots)]
    middles = []
    for s in range(slots):
        grad = jnp.concatenate(
            [(mm(coded[s][:, c:c + 256], signs) * NORM).astype(BF) for c in range(0, width, 256)], axis=1)
        grad_ref[s] = grad
        middles.append(mm_t(grad, rroot_ref[s]).astype(BF))
    for s in range(slots):
        for k, ref in enumerate((hops_ref, swapped_ref)):
            left = ref[:, s * slab:(s + 1) * slab, :].reshape(groups * slab, width)
            rows = mm(left, middles[s]).astype(BF)
            for d in range(groups):
                start = ((chip + groups - d) % groups * 2 + (core + k) % 2) * slab
                out_ref[pl.ds(pl.multiple_of(start, slab), slab), s * slab:(s + 1) * slab] = (
                    rows[d * slab:(d + 1) * slab])


def kernel_params():
    return pltpu.CompilerParams(vmem_limit_bytes=VMEM_BYTES)


def in_vmem():
    return pl.BlockSpec(memory_space=pltpu.VMEM)


def code_call(x, nrep):
    nb, rows, width = x.shape
    per = rows * width // GROUP // nrep
    return pl.pallas_call(
        code_kernel,
        out_shape=jax.ShapeDtypeStruct((nrep, nb * per, GROUP), BF),
        in_specs=[in_vmem()],
        out_specs=in_vmem(),
        compiler_params=kernel_params(),
    )(x)


def route_call(got, route):
    return pl.pallas_call(
        route_kernel,
        out_shape=jax.ShapeDtypeStruct((route.shape[0], got.shape[2]), BF),
        in_specs=[in_vmem()] * 2,
        out_specs=in_vmem(),
        compiler_params=kernel_params(),
    )(got, route)


def pick_call(back, pick, rows):
    nb = pick.shape[2] // rows
    return pl.pallas_call(
        pick_kernel,
        out_shape=jax.ShapeDtypeStruct((rows, back.shape[1] // SLOTS, nb), BF),
        in_specs=[in_vmem()] * 2,
        out_specs=in_vmem(),
        compiler_params=kernel_params(),
    )(back, pick)


def root_call(rank, mine, other, hops, swapped, rroot):
    slots, slab, width = rroot.shape
    return pl.pallas_call(
        root_kernel,
        out_shape=(jax.ShapeDtypeStruct((slots, width, width), BF),
                   jax.ShapeDtypeStruct((width, slots * slab), BF)),
        in_specs=[pl.BlockSpec(memory_space=pltpu.SMEM)] + [in_vmem()] * 5,
        out_specs=(in_vmem(), in_vmem()),
        compiler_params=kernel_params(),
    )(rank, mine, other, hops, swapped, rroot)


def on_device(grads, owner, left_stat, right_stat, left_root, right_root):
    x = grads[0]
    nb, rows, width = x.shape
    nx, nz = lax.axis_size("x"), lax.axis_size("z")
    nf = nx * nz
    halves = lax.axis_size("core")
    groups = lax.axis_size("y")
    nrep = groups * halves
    per = rows // halves
    slab = width // nrep
    rank = lax.axis_index(REP)

    got = lax.all_to_all(code_call(x, nrep), REP, split_axis=0, concat_axis=0, tiled=True)

    counter = jnp.arange(nb, dtype=I32)
    same = owner[:, None] == owner[None, :]
    slot_of = jnp.sum(same & (counter[None, :] < counter[:, None]), axis=1)
    place = ((owner % nz) * nx + owner // nz) * SLOTS + slot_of
    key_in = jnp.concatenate([place * per + r for r in range(per)])
    route = (jnp.arange(nf * SLOTS * per, dtype=I32)[:, None] == key_in[None, :]).astype(BF)
    outgoing = route_call(got, route).reshape(nz, nx * SLOTS * per, GROUP)

    outgoing, own = lax.optimization_barrier((outgoing, left_root[0]))
    arrived = lax.all_to_all(outgoing, "z", split_axis=0, concat_axis=0, tiled=True)
    own = own.reshape(SLOTS * slab, width)
    hops = [own]
    for d in range(1, groups):
        hops.append(lax.ppermute(own, "y", [(j, (j + d) % groups) for j in range(groups)]))
    arrived, hops = lax.optimization_barrier((arrived, hops))
    swap = [(0, 1), (1, 0)]
    hops = jnp.stack(hops)
    swapped = lax.ppermute(hops, "core", swap)

    tile = nz * SLOTS * per
    pieces = arrived.reshape(nz, nx, SLOTS * per, GROUP).transpose(1, 0, 2, 3).reshape(nx, 1, tile, GROUP)
    copies = jnp.broadcast_to(pieces, (nx, groups, tile, GROUP)).reshape(nx * groups, tile, GROUP)
    mine = lax.all_to_all(copies, ("x", "y"), split_axis=0, concat_axis=0, tiled=True)
    other = lax.ppermute(mine, "core", swap)
    gradient, direction = root_call(rank.reshape(1), mine, other, hops, swapped, right_root[0])
    packed = direction.reshape(nf, rows, SLOTS * slab)
    back = lax.all_to_all(packed, FSDP, split_axis=0, concat_axis=0, tiled=True)

    own_rows = lax.dynamic_slice_in_dim(gradient, rank * slab, slab, axis=1)
    own_cols = lax.dynamic_slice_in_dim(gradient, rank * slab, slab, axis=2)
    left_gram = jnp.einsum("sik,sjk->sij", own_rows, gradient, preferred_element_type=F32)
    right_gram = jnp.einsum("ski,skj->sij", own_cols, gradient, preferred_element_type=F32)
    left_new = DECAY * left_stat[0] + (1 - DECAY) * left_gram
    right_new = DECAY * right_stat[0] + (1 - DECAY) * right_gram

    owner_row = jnp.arange(nf * rows, dtype=I32)
    pick = []
    for s in range(SLOTS):
        key = jnp.where(slot_of == s, owner * rows, -rows)
        key = jnp.concatenate([key + r for r in range(rows)])
        pick.append((owner_row[:, None] == key[None, :]).astype(BF))
    update = pick_call(back.reshape(nf * rows, SLOTS * slab), jnp.stack(pick), rows).transpose(2, 0, 1)
    return (left_new[None], right_new[None], update)


def solution(mesh):
    nz = 32
    nf, nrep = mesh.shape["fsdp"], mesh.shape["rep"]
    mesh = Mesh(mesh.devices.reshape(nf // nz, nz, nrep // 2, 2), FSDP + REP)
    held = P(FSDP, None, REP, None)
    return jax.shard_map(
        on_device, mesh=mesh, in_specs=(P(REP, None, FSDP, None), P(), held, held, held, held),
        out_specs=(held, held, P(None, FSDP, REP)), check_vma=False)
```

```python
import jax
import jax.numpy as jnp
from jax import lax
from jax.experimental import pallas as pl
from jax.experimental.pallas import tpu as pltpu
from jax.sharding import Mesh, PartitionSpec as P

GROUP = 128
SLOTS = 2
FAR = (16, 16)
FSDP, REP = ("x", "z"), ("y", "core")
DECAY = 0.95
NORM = GROUP ** (-0.5)
BF, F32, I32 = jnp.bfloat16, jnp.float32, jnp.int32
VMEM_BYTES = 24 * 1024 * 1024


def hadamard():
    i = lax.broadcasted_iota(I32, (GROUP, GROUP), 0)
    j = lax.broadcasted_iota(I32, (GROUP, GROUP), 1)
    bits = i & j
    parity = jnp.zeros((GROUP, GROUP), I32)
    for k in range(GROUP.bit_length() - 1):
        parity = parity ^ ((bits >> k) & 1)
    return (1 - 2 * parity).astype(F32).astype(BF)


def mm(a, b):
    return jnp.dot(a, b, preferred_element_type=F32)


def mm_t(a, b):
    return lax.dot_general(a, b, (((1,), (1,)), ((), ())), preferred_element_type=F32)


def code_kernel(x_ref, out_ref):
    blocks, rows, width = x_ref.shape
    nrep, _, _ = out_ref.shape
    groups = width // GROUP
    halves = nrep // groups
    per = rows // halves
    signs = hadamard()
    step = 256 // rows
    o = lax.broadcasted_iota(I32, (256, 256), 0)
    i = lax.broadcasted_iota(I32, (256, 256), 1)
    perm = ((i // rows == o % step) & (i % rows == o // step)).astype(F32).astype(BF)
    for t in range(blocks // step):
        x = x_ref[t * step:(t + 1) * step].reshape(256, width)
        x = mm(perm, x).astype(BF)
        for g in range(groups):
            turned = mm(x[:, g * GROUP:(g + 1) * GROUP], signs) * NORM
            peak = jnp.max(jnp.abs(turned), axis=1, keepdims=True) + 1e-06
            scale = peak.astype(BF).astype(F32)
            codes = (turned / scale).astype(BF).astype(F32)
            terms = (codes * scale).astype(BF)
            for h in range(halves):
                for r in range(per):
                    row = (h * per + r) * step
                    out_ref[g * halves + h, r * blocks + t * step:r * blocks + (t + 1) * step, :] = (
                        terms[row:row + step])


def route_kernel(got_ref, route_ref, out_ref):
    total = got_ref[0].astype(F32)
    for k in range(1, got_ref.shape[0]):
        total += got_ref[k].astype(F32)
    out_ref[...] = mm(route_ref[...], total.astype(BF)).astype(BF)


def pick_kernel(back_ref, pick_ref, out_ref):
    rows, slab, blocks = out_ref.shape
    back = back_ref[...].astype(F32).T.astype(BF)
    total = mm(back[:slab], pick_ref[0]) + mm(back[slab:], pick_ref[1])
    for r in range(rows):
        out_ref[r] = total[:, r * blocks:(r + 1) * blocks].astype(BF)


def root_kernel(rank_ref, mine_ref, other_ref, hops_ref, swapped_ref, rroot_ref, grad_ref, out_ref):
    groups = hops_ref.shape[0]
    slots, width, _ = grad_ref.shape
    slab = rroot_ref.shape[1]
    rank = rank_ref[0]
    core = rank % 2
    chip = rank // 2
    one = hadamard()
    none = jnp.zeros_like(one)
    signs = jnp.concatenate([jnp.concatenate([one, none], axis=1), jnp.concatenate([none, one], axis=1)], axis=0)
    o = lax.broadcasted_iota(I32, (256, 256), 0)
    i = lax.broadcasted_iota(I32, (256, 256), 1)
    half = jnp.where(i < 128, core, 1 - core)
    from_row = (((i % 128) // 4) ^ FAR[0]) * 4 + half * 2 + i % 2
    perm = ((o % 128 == from_row) & (o // 128 == (i // 2) % 2)).astype(F32).astype(BF)
    tiles = width // 128
    placed = []
    for t in range(tiles):
        both = jnp.concatenate([
            jnp.concatenate([ref[t * groups + g] for g in range(groups)], axis=1) for ref in (mine_ref, other_ref)], axis=0)
        placed.append(mm(perm, both).astype(BF))
    coded = [jnp.concatenate([p[s * 128:(s + 1) * 128] for p in placed], axis=0) for s in range(slots)]
    middles = []
    for s in range(slots):
        grad = jnp.concatenate(
            [(mm(coded[s][:, c:c + 256], signs) * NORM).astype(BF) for c in range(0, width, 256)], axis=1)
        grad_ref[s] = grad
        middles.append(mm_t(grad, rroot_ref[s]).astype(BF))
    for s in range(slots):
        for k, ref in enumerate((hops_ref, swapped_ref)):
            left = ref[:, s * slab:(s + 1) * slab, :].reshape(groups * slab, width)
            rows = mm(left, middles[s]).astype(BF)
            for d in range(groups):
                start = ((chip + groups - d) % groups * 2 + (core + k + FAR[1] // 16) % 2) * slab
                out_ref[pl.ds(pl.multiple_of(start, slab), slab), s * slab:(s + 1) * slab] = (
                    rows[d * slab:(d + 1) * slab])


def kernel_params():
    return pltpu.CompilerParams(vmem_limit_bytes=VMEM_BYTES)


def in_vmem():
    return pl.BlockSpec(memory_space=pltpu.VMEM)


def code_call(x, nrep):
    nb, rows, width = x.shape
    per = rows * width // GROUP // nrep
    return pl.pallas_call(
        code_kernel,
        out_shape=jax.ShapeDtypeStruct((nrep, nb * per, GROUP), BF),
        in_specs=[in_vmem()],
        out_specs=in_vmem(),
        compiler_params=kernel_params(),
    )(x)


def route_call(got, route):
    return pl.pallas_call(
        route_kernel,
        out_shape=jax.ShapeDtypeStruct((route.shape[0], got.shape[2]), BF),
        in_specs=[in_vmem()] * 2,
        out_specs=in_vmem(),
        compiler_params=kernel_params(),
    )(got, route)


def pick_call(back, pick, rows):
    nb = pick.shape[2] // rows
    return pl.pallas_call(
        pick_kernel,
        out_shape=jax.ShapeDtypeStruct((rows, back.shape[1] // SLOTS, nb), BF),
        in_specs=[in_vmem()] * 2,
        out_specs=in_vmem(),
        compiler_params=kernel_params(),
    )(back, pick)


def root_call(rank, mine, other, hops, swapped, rroot):
    slots, slab, width = rroot.shape
    return pl.pallas_call(
        root_kernel,
        out_shape=(jax.ShapeDtypeStruct((slots, width, width), BF),
                   jax.ShapeDtypeStruct((width, slots * slab), BF)),
        in_specs=[pl.BlockSpec(memory_space=pltpu.SMEM)] + [in_vmem()] * 5,
        out_specs=(in_vmem(), in_vmem()),
        compiler_params=kernel_params(),
    )(rank, mine, other, hops, swapped, rroot)


def on_device(grads, owner, left_stat, right_stat, left_root, right_root):
    x = grads[0]
    nb, rows, width = x.shape
    nx, nz = lax.axis_size("x"), lax.axis_size("z")
    nf = nx * nz
    halves = lax.axis_size("core")
    groups = lax.axis_size("y")
    nrep = groups * halves
    per = rows // halves
    slab = width // nrep
    rank = lax.axis_index(REP)

    got = lax.all_to_all(code_call(x, nrep), REP, split_axis=0, concat_axis=0, tiled=True)

    counter = jnp.arange(nb, dtype=I32)
    same = owner[:, None] == owner[None, :]
    slot_of = jnp.sum(same & (counter[None, :] < counter[:, None]), axis=1)
    place = (((owner ^ FAR[0]) % nz) * nx + owner // nz) * SLOTS + slot_of
    key_in = jnp.concatenate([place * per + r for r in range(per)])
    route = (jnp.arange(nf * SLOTS * per, dtype=I32)[:, None] == key_in[None, :]).astype(BF)
    outgoing = route_call(got, route).reshape(nz, nx * SLOTS * per, GROUP)

    outgoing, own = lax.optimization_barrier((outgoing, left_root[0]))
    arrived = lax.all_to_all(outgoing, "z", split_axis=0, concat_axis=0, tiled=True,
                             axis_index_groups=[[p ^ FAR[0] for p in range(nz)]])
    own = own.reshape(SLOTS * slab, width)
    hops = [own]
    for d in range(1, groups):
        hops.append(lax.ppermute(own, "y", [(j, (j + d) % groups) for j in range(groups)]))
    arrived, hops = lax.optimization_barrier((arrived, hops))
    swap = [(0, 1), (1, 0)]
    hops = jnp.stack(hops)
    swapped = lax.ppermute(hops, "core", swap)

    tile = nz * SLOTS * per
    pieces = arrived.reshape(nz, nx, SLOTS * per, GROUP).transpose(1, 0, 2, 3).reshape(nx, 1, tile, GROUP)
    copies = jnp.broadcast_to(pieces, (nx, groups, tile, GROUP)).reshape(nx * groups, tile, GROUP)
    mine = lax.all_to_all(copies, ("x", "y"), split_axis=0, concat_axis=0, tiled=True)
    other = lax.ppermute(mine, "core", swap)
    gradient, direction = root_call(rank.reshape(1), mine, other, hops, swapped, right_root[0])
    packed = direction.reshape(nf, rows, SLOTS * slab)
    back = lax.all_to_all(packed, FSDP, split_axis=0, concat_axis=0, tiled=True,
                          axis_index_groups=[[p ^ FAR[1] for p in range(nf)]])

    own_rows = lax.dynamic_slice_in_dim(gradient, rank * slab, slab, axis=1)
    own_cols = lax.dynamic_slice_in_dim(gradient, rank * slab, slab, axis=2)
    left_gram = jnp.einsum("sik,sjk->sij", own_rows, gradient, preferred_element_type=F32)
    right_gram = jnp.einsum("ski,skj->sij", own_cols, gradient, preferred_element_type=F32)
    left_new = DECAY * left_stat[0] + (1 - DECAY) * left_gram
    right_new = DECAY * right_stat[0] + (1 - DECAY) * right_gram

    owner_row = jnp.arange(nf * rows, dtype=I32)
    pick = []
    for s in range(SLOTS):
        key = jnp.where(slot_of == s, (owner ^ FAR[1]) * rows, -rows)
        key = jnp.concatenate([key + r for r in range(rows)])
        pick.append((owner_row[:, None] == key[None, :]).astype(BF))
    update = pick_call(back.reshape(nf * rows, SLOTS * slab), jnp.stack(pick), rows).transpose(2, 0, 1)
    return (left_new[None], right_new[None], update)


def solution(mesh):
    nz = 32
    nf, nrep = mesh.shape["fsdp"], mesh.shape["rep"]
    mesh = Mesh(mesh.devices.reshape(nf // nz, nz, nrep // 2, 2), FSDP + REP)
    held = P(FSDP, None, REP, None)
    return jax.shard_map(
        on_device, mesh=mesh, in_specs=(P(REP, None, FSDP, None), P(), held, held, held, held),
        out_specs=(held, held, P(None, FSDP, REP)), check_vma=False)
```

```python
import jax
import jax.numpy as jnp
from jax import lax
from jax.experimental import pallas as pl
from jax.experimental.pallas import tpu as pltpu
from jax.sharding import Mesh, PartitionSpec as P

GROUP = 128
SLOTS = 2
FAR = (20, 20)
FSDP, REP = ("x", "z"), ("y", "core")
DECAY = 0.95
NORM = GROUP ** (-0.5)
BF, F32, I32 = jnp.bfloat16, jnp.float32, jnp.int32
VMEM_BYTES = 24 * 1024 * 1024


def hadamard():
    i = lax.broadcasted_iota(I32, (GROUP, GROUP), 0)
    j = lax.broadcasted_iota(I32, (GROUP, GROUP), 1)
    bits = i & j
    parity = jnp.zeros((GROUP, GROUP), I32)
    for k in range(GROUP.bit_length() - 1):
        parity = parity ^ ((bits >> k) & 1)
    return (1 - 2 * parity).astype(F32).astype(BF)


def mm(a, b):
    return jnp.dot(a, b, preferred_element_type=F32)


def mm_t(a, b):
    return lax.dot_general(a, b, (((1,), (1,)), ((), ())), preferred_element_type=F32)


def code_kernel(x_ref, out_ref):
    blocks, rows, width = x_ref.shape
    nrep, _, _ = out_ref.shape
    groups = width // GROUP
    halves = nrep // groups
    per = rows // halves
    signs = hadamard()
    step = 256 // rows
    o = lax.broadcasted_iota(I32, (256, 256), 0)
    i = lax.broadcasted_iota(I32, (256, 256), 1)
    perm = ((i // rows == o % step) & (i % rows == o // step)).astype(F32).astype(BF)
    for t in range(blocks // step):
        x = x_ref[t * step:(t + 1) * step].reshape(256, width)
        x = mm(perm, x).astype(BF)
        for g in range(groups):
            turned = mm(x[:, g * GROUP:(g + 1) * GROUP], signs) * NORM
            peak = jnp.max(jnp.abs(turned), axis=1, keepdims=True) + 1e-06
            scale = peak.astype(BF).astype(F32)
            codes = (turned / scale).astype(BF).astype(F32)
            terms = (codes * scale).astype(BF)
            for h in range(halves):
                for r in range(per):
                    row = (h * per + r) * step
                    out_ref[g * halves + h, r * blocks + t * step:r * blocks + (t + 1) * step, :] = (
                        terms[row:row + step])


def route_kernel(got_ref, route_ref, out_ref):
    total = got_ref[0].astype(F32)
    for k in range(1, got_ref.shape[0]):
        total += got_ref[k].astype(F32)
    out_ref[...] = mm(route_ref[...], total.astype(BF)).astype(BF)


def pick_kernel(back_ref, pick_ref, out_ref):
    rows, slab, blocks = out_ref.shape
    back = back_ref[...].astype(F32).T.astype(BF)
    total = mm(back[:slab], pick_ref[0]) + mm(back[slab:], pick_ref[1])
    for r in range(rows):
        out_ref[r] = total[:, r * blocks:(r + 1) * blocks].astype(BF)


def root_kernel(rank_ref, mine_ref, other_ref, hops_ref, swapped_ref, rroot_ref, grad_ref, out_ref):
    groups = hops_ref.shape[0]
    slots, width, _ = grad_ref.shape
    slab = rroot_ref.shape[1]
    rank = rank_ref[0]
    core = rank % 2
    chip = rank // 2
    one = hadamard()
    none = jnp.zeros_like(one)
    signs = jnp.concatenate([jnp.concatenate([one, none], axis=1), jnp.concatenate([none, one], axis=1)], axis=0)
    o = lax.broadcasted_iota(I32, (256, 256), 0)
    i = lax.broadcasted_iota(I32, (256, 256), 1)
    half = jnp.where(i < 128, core, 1 - core)
    from_row = (((i % 128) // 4) ^ FAR[0]) * 4 + half * 2 + i % 2
    perm = ((o % 128 == from_row) & (o // 128 == (i // 2) % 2)).astype(F32).astype(BF)
    tiles = width // 128
    placed = []
    for t in range(tiles):
        both = jnp.concatenate([
            jnp.concatenate([ref[t * groups + g] for g in range(groups)], axis=1) for ref in (mine_ref, other_ref)], axis=0)
        placed.append(mm(perm, both).astype(BF))
    coded = [jnp.concatenate([p[s * 128:(s + 1) * 128] for p in placed], axis=0) for s in range(slots)]
    middles = []
    for s in range(slots):
        grad = jnp.concatenate(
            [(mm(coded[s][:, c:c + 256], signs) * NORM).astype(BF) for c in range(0, width, 256)], axis=1)
        grad_ref[s] = grad
        middles.append(mm_t(grad, rroot_ref[s]).astype(BF))
    for s in range(slots):
        for k, ref in enumerate((hops_ref, swapped_ref)):
            left = ref[:, s * slab:(s + 1) * slab, :].reshape(groups * slab, width)
            rows = mm(left, middles[s]).astype(BF)
            for d in range(groups):
                start = ((chip + groups - d) % groups * 2 + (core + k + FAR[1] // 16) % 2) * slab
                for b in range(slab // 16):
                    place = pl.multiple_of(start + (b ^ (FAR[1] % 16 // 4)) * 16, 16)
                    out_ref[pl.ds(place, 16), s * slab:(s + 1) * slab] = rows[d * slab + b * 16:d * slab + (b + 1) * 16]


def kernel_params():
    return pltpu.CompilerParams(vmem_limit_bytes=VMEM_BYTES)


def in_vmem():
    return pl.BlockSpec(memory_space=pltpu.VMEM)


def code_call(x, nrep):
    nb, rows, width = x.shape
    per = rows * width // GROUP // nrep
    return pl.pallas_call(
        code_kernel,
        out_shape=jax.ShapeDtypeStruct((nrep, nb * per, GROUP), BF),
        in_specs=[in_vmem()],
        out_specs=in_vmem(),
        compiler_params=kernel_params(),
    )(x)


def route_call(got, route):
    return pl.pallas_call(
        route_kernel,
        out_shape=jax.ShapeDtypeStruct((route.shape[0], got.shape[2]), BF),
        in_specs=[in_vmem()] * 2,
        out_specs=in_vmem(),
        compiler_params=kernel_params(),
    )(got, route)


def pick_call(back, pick, rows):
    nb = pick.shape[2] // rows
    return pl.pallas_call(
        pick_kernel,
        out_shape=jax.ShapeDtypeStruct((rows, back.shape[1] // SLOTS, nb), BF),
        in_specs=[in_vmem()] * 2,
        out_specs=in_vmem(),
        compiler_params=kernel_params(),
    )(back, pick)


def root_call(rank, mine, other, hops, swapped, rroot):
    slots, slab, width = rroot.shape
    return pl.pallas_call(
        root_kernel,
        out_shape=(jax.ShapeDtypeStruct((slots, width, width), BF),
                   jax.ShapeDtypeStruct((width, slots * slab), BF)),
        in_specs=[pl.BlockSpec(memory_space=pltpu.SMEM)] + [in_vmem()] * 5,
        out_specs=(in_vmem(), in_vmem()),
        compiler_params=kernel_params(),
    )(rank, mine, other, hops, swapped, rroot)


def on_device(grads, owner, left_stat, right_stat, left_root, right_root):
    x = grads[0]
    nb, rows, width = x.shape
    nx, nz = lax.axis_size("x"), lax.axis_size("z")
    nf = nx * nz
    halves = lax.axis_size("core")
    groups = lax.axis_size("y")
    nrep = groups * halves
    per = rows // halves
    slab = width // nrep
    rank = lax.axis_index(REP)

    got = lax.all_to_all(code_call(x, nrep), REP, split_axis=0, concat_axis=0, tiled=True)

    counter = jnp.arange(nb, dtype=I32)
    same = owner[:, None] == owner[None, :]
    slot_of = jnp.sum(same & (counter[None, :] < counter[:, None]), axis=1)
    place = (((owner ^ FAR[0]) % nz) * nx + owner // nz) * SLOTS + slot_of
    key_in = jnp.concatenate([place * per + r for r in range(per)])
    route = (jnp.arange(nf * SLOTS * per, dtype=I32)[:, None] == key_in[None, :]).astype(BF)
    outgoing = route_call(got, route).reshape(nz, nx * SLOTS * per, GROUP)

    outgoing, own = lax.optimization_barrier((outgoing, left_root[0]))
    arrived = lax.all_to_all(outgoing, "z", split_axis=0, concat_axis=0, tiled=True,
                             axis_index_groups=[[p ^ FAR[0] for p in range(nz)]])
    own = own.reshape(SLOTS * slab, width)
    hops = [own]
    for d in range(1, groups):
        hops.append(lax.ppermute(own, "y", [(j, (j + d) % groups) for j in range(groups)]))
    arrived, hops = lax.optimization_barrier((arrived, hops))
    swap = [(0, 1), (1, 0)]
    hops = jnp.stack(hops)
    swapped = lax.ppermute(hops, "core", swap)

    tile = nz * SLOTS * per
    pieces = arrived.reshape(nz, nx, SLOTS * per, GROUP).transpose(1, 0, 2, 3).reshape(nx, 1, tile, GROUP)
    copies = jnp.broadcast_to(pieces, (nx, groups, tile, GROUP)).reshape(nx * groups, tile, GROUP)
    mine = lax.all_to_all(copies, ("x", "y"), split_axis=0, concat_axis=0, tiled=True)
    other = lax.ppermute(mine, "core", swap)
    gradient, direction = root_call(rank.reshape(1), mine, other, hops, swapped, right_root[0])
    packed = direction.reshape(nf, rows, SLOTS * slab)
    back = lax.all_to_all(packed, FSDP, split_axis=0, concat_axis=0, tiled=True,
                          axis_index_groups=[[p ^ FAR[1] for p in range(nf)]])

    own_rows = lax.dynamic_slice_in_dim(gradient, rank * slab, slab, axis=1)
    own_cols = lax.dynamic_slice_in_dim(gradient, rank * slab, slab, axis=2)
    left_gram = jnp.einsum("sik,sjk->sij", own_rows, gradient, preferred_element_type=F32)
    right_gram = jnp.einsum("ski,skj->sij", own_cols, gradient, preferred_element_type=F32)
    left_new = DECAY * left_stat[0] + (1 - DECAY) * left_gram
    right_new = DECAY * right_stat[0] + (1 - DECAY) * right_gram

    owner_row = jnp.arange(nf * rows, dtype=I32)
    pick = []
    for s in range(SLOTS):
        key = jnp.where(slot_of == s, (owner ^ FAR[1]) * rows, -rows)
        key = jnp.concatenate([key + r for r in range(rows)])
        pick.append((owner_row[:, None] == key[None, :]).astype(BF))
    update = pick_call(back.reshape(nf * rows, SLOTS * slab), jnp.stack(pick), rows).transpose(2, 0, 1)
    return (left_new[None], right_new[None], update)


def solution(mesh):
    nz = 32
    nf, nrep = mesh.shape["fsdp"], mesh.shape["rep"]
    mesh = Mesh(mesh.devices.reshape(nf // nz, nz, nrep // 2, 2), FSDP + REP)
    held = P(FSDP, None, REP, None)
    return jax.shard_map(
        on_device, mesh=mesh, in_specs=(P(REP, None, FSDP, None), P(), held, held, held, held),
        out_specs=(held, held, P(None, FSDP, REP)), check_vma=False)
```

```python
import jax
import jax.numpy as jnp
from jax import lax
from jax.experimental import pallas as pl
from jax.experimental.pallas import tpu as pltpu
from jax.sharding import Mesh, PartitionSpec as P

GROUP = 128
SLOTS = 2
FAR = (20, 20)
FSDP, REP = ("x", "z"), ("y", "core")
DECAY = 0.95
NORM = GROUP ** (-0.5)
BF, F32, I32 = jnp.bfloat16, jnp.float32, jnp.int32
VMEM_BYTES = 24 * 1024 * 1024


def hadamard():
    i = lax.broadcasted_iota(I32, (GROUP, GROUP), 0)
    j = lax.broadcasted_iota(I32, (GROUP, GROUP), 1)
    bits = i & j
    parity = jnp.zeros((GROUP, GROUP), I32)
    for k in range(GROUP.bit_length() - 1):
        parity = parity ^ ((bits >> k) & 1)
    return (1 - 2 * parity).astype(F32).astype(BF)


def mm(a, b):
    return jnp.dot(a, b, preferred_element_type=F32)


def mm_t(a, b):
    return lax.dot_general(a, b, (((1,), (1,)), ((), ())), preferred_element_type=F32)


def code_kernel(x_ref, out_ref):
    blocks, rows, width = x_ref.shape
    nrep, _, _ = out_ref.shape
    groups = width // GROUP
    halves = nrep // groups
    per = rows // halves
    signs = hadamard()
    step = 256 // rows
    o = lax.broadcasted_iota(I32, (256, 256), 0)
    i = lax.broadcasted_iota(I32, (256, 256), 1)
    perm = ((i // rows == o % step) & (i % rows == o // step)).astype(F32).astype(BF)
    for t in range(blocks // step):
        x = x_ref[t * step:(t + 1) * step].reshape(256, width)
        x = mm(perm, x).astype(BF)
        for g in range(groups):
            turned = mm(x[:, g * GROUP:(g + 1) * GROUP], signs) * NORM
            peak = jnp.max(jnp.abs(turned), axis=1, keepdims=True) + 1e-06
            scale = peak.astype(BF).astype(F32)
            codes = (turned / scale).astype(BF).astype(F32)
            terms = (codes * scale).astype(BF)
            for h in range(halves):
                for r in range(per):
                    row = (h * per + r) * step
                    out_ref[(g * halves + h) ^ (nrep // 2), r * blocks + t * step:r * blocks + (t + 1) * step, :] = (
                        terms[row:row + step])


def route_kernel(got_ref, route_ref, out_ref):
    total = got_ref[0].astype(F32)
    for k in range(1, got_ref.shape[0]):
        total += got_ref[k].astype(F32)
    out_ref[...] = mm(route_ref[...], total.astype(BF)).astype(BF)


def pick_kernel(back_ref, pick_ref, out_ref):
    rows, slab, blocks = out_ref.shape
    back = back_ref[...].astype(F32).T.astype(BF)
    total = mm(back[:slab], pick_ref[0]) + mm(back[slab:], pick_ref[1])
    for r in range(rows):
        out_ref[r] = total[:, r * blocks:(r + 1) * blocks].astype(BF)


def root_kernel(rank_ref, mine_ref, other_ref, hops_ref, swapped_ref, rroot_ref, grad_ref, out_ref):
    groups = hops_ref.shape[0]
    slots, width, _ = grad_ref.shape
    slab = rroot_ref.shape[1]
    rank = rank_ref[0]
    core = rank % 2
    chip = rank // 2
    one = hadamard()
    none = jnp.zeros_like(one)
    signs = jnp.concatenate([jnp.concatenate([one, none], axis=1), jnp.concatenate([none, one], axis=1)], axis=0)
    o = lax.broadcasted_iota(I32, (256, 256), 0)
    i = lax.broadcasted_iota(I32, (256, 256), 1)
    half = jnp.where(i < 128, core, 1 - core)
    from_row = (((i % 128) // 4) ^ FAR[0]) * 4 + half * 2 + i % 2
    perm = ((o % 128 == from_row) & (o // 128 == (i // 2) % 2)).astype(F32).astype(BF)
    tiles = width // 128
    placed = []
    for t in range(tiles):
        both = jnp.concatenate([
            jnp.concatenate([ref[t * groups + g] for g in range(groups)], axis=1) for ref in (mine_ref, other_ref)], axis=0)
        placed.append(mm(perm, both).astype(BF))
    coded = [jnp.concatenate([p[s * 128:(s + 1) * 128] for p in placed], axis=0) for s in range(slots)]
    middles = []
    for s in range(slots):
        grad = jnp.concatenate(
            [(mm(coded[s][:, c:c + 256], signs) * NORM).astype(BF) for c in range(0, width, 256)], axis=1)
        grad_ref[s] = grad
        middles.append(mm_t(grad, rroot_ref[s]).astype(BF))
    for s in range(slots):
        for k, ref in enumerate((hops_ref, swapped_ref)):
            left = ref[:, s * slab:(s + 1) * slab, :].reshape(groups * slab, width)
            rows = mm(left, middles[s]).astype(BF)
            for d in range(groups):
                start = ((chip + groups - d) % groups * 2 + (core + k + FAR[1] // 16) % 2) * slab
                for b in range(slab // 16):
                    place = pl.multiple_of(start + (b ^ (FAR[1] % 16 // 4)) * 16, 16)
                    out_ref[pl.ds(place, 16), s * slab:(s + 1) * slab] = rows[d * slab + b * 16:d * slab + (b + 1) * 16]


def kernel_params():
    return pltpu.CompilerParams(vmem_limit_bytes=VMEM_BYTES)


def in_vmem():
    return pl.BlockSpec(memory_space=pltpu.VMEM)


def code_call(x, nrep):
    nb, rows, width = x.shape
    per = rows * width // GROUP // nrep
    return pl.pallas_call(
        code_kernel,
        out_shape=jax.ShapeDtypeStruct((nrep, nb * per, GROUP), BF),
        in_specs=[in_vmem()],
        out_specs=in_vmem(),
        compiler_params=kernel_params(),
    )(x)


def route_call(got, route):
    return pl.pallas_call(
        route_kernel,
        out_shape=jax.ShapeDtypeStruct((route.shape[0], got.shape[2]), BF),
        in_specs=[in_vmem()] * 2,
        out_specs=in_vmem(),
        compiler_params=kernel_params(),
    )(got, route)


def pick_call(back, pick, rows):
    nb = pick.shape[2] // rows
    return pl.pallas_call(
        pick_kernel,
        out_shape=jax.ShapeDtypeStruct((rows, back.shape[1] // SLOTS, nb), BF),
        in_specs=[in_vmem()] * 2,
        out_specs=in_vmem(),
        compiler_params=kernel_params(),
    )(back, pick)


def root_call(rank, mine, other, hops, swapped, rroot):
    slots, slab, width = rroot.shape
    return pl.pallas_call(
        root_kernel,
        out_shape=(jax.ShapeDtypeStruct((slots, width, width), BF),
                   jax.ShapeDtypeStruct((width, slots * slab), BF)),
        in_specs=[pl.BlockSpec(memory_space=pltpu.SMEM)] + [in_vmem()] * 5,
        out_specs=(in_vmem(), in_vmem()),
        compiler_params=kernel_params(),
    )(rank, mine, other, hops, swapped, rroot)


def on_device(grads, owner, left_stat, right_stat, left_root, right_root):
    x = grads[0]
    nb, rows, width = x.shape
    nx, nz = lax.axis_size("x"), lax.axis_size("z")
    nf = nx * nz
    halves = lax.axis_size("core")
    groups = lax.axis_size("y")
    nrep = groups * halves
    per = rows // halves
    slab = width // nrep
    rank = lax.axis_index(REP)

    got = lax.all_to_all(code_call(x, nrep), REP, split_axis=0, concat_axis=0, tiled=True,
                         axis_index_groups=[[p ^ (nrep // 2) for p in range(nrep)]])

    counter = jnp.arange(nb, dtype=I32)
    same = owner[:, None] == owner[None, :]
    slot_of = jnp.sum(same & (counter[None, :] < counter[:, None]), axis=1)
    place = (((owner ^ FAR[0]) % nz) * nx + owner // nz) * SLOTS + slot_of
    key_in = jnp.concatenate([place * per + r for r in range(per)])
    route = (jnp.arange(nf * SLOTS * per, dtype=I32)[:, None] == key_in[None, :]).astype(BF)
    outgoing = route_call(got, route).reshape(nz, nx * SLOTS * per, GROUP)

    outgoing, own = lax.optimization_barrier((outgoing, left_root[0]))
    arrived = lax.all_to_all(outgoing, "z", split_axis=0, concat_axis=0, tiled=True,
                             axis_index_groups=[[p ^ FAR[0] for p in range(nz)]])
    own = own.reshape(SLOTS * slab, width)
    hops = [own]
    for d in range(1, groups):
        hops.append(lax.ppermute(own, "y", [(j, (j + d) % groups) for j in range(groups)]))
    arrived, hops = lax.optimization_barrier((arrived, hops))
    swap = [(0, 1), (1, 0)]
    hops = jnp.stack(hops)
    swapped = lax.ppermute(hops, "core", swap)

    tile = nz * SLOTS * per
    pieces = arrived.reshape(nz, nx, SLOTS * per, GROUP).transpose(1, 0, 2, 3).reshape(nx, 1, tile, GROUP)
    copies = jnp.broadcast_to(pieces, (nx, groups, tile, GROUP)).reshape(nx * groups, tile, GROUP)
    mine = lax.all_to_all(copies, ("x", "y"), split_axis=0, concat_axis=0, tiled=True)
    other = lax.ppermute(mine, "core", swap)
    gradient, direction = root_call(rank.reshape(1), mine, other, hops, swapped, right_root[0])
    packed = direction.reshape(nf, rows, SLOTS * slab)
    back = lax.all_to_all(packed, FSDP, split_axis=0, concat_axis=0, tiled=True,
                          axis_index_groups=[[p ^ FAR[1] for p in range(nf)]])

    own_rows = lax.dynamic_slice_in_dim(gradient, rank * slab, slab, axis=1)
    own_cols = lax.dynamic_slice_in_dim(gradient, rank * slab, slab, axis=2)
    left_gram = jnp.einsum("sik,sjk->sij", own_rows, gradient, preferred_element_type=F32)
    right_gram = jnp.einsum("ski,skj->sij", own_cols, gradient, preferred_element_type=F32)
    left_new = DECAY * left_stat[0] + (1 - DECAY) * left_gram
    right_new = DECAY * right_stat[0] + (1 - DECAY) * right_gram

    owner_row = jnp.arange(nf * rows, dtype=I32)
    pick = []
    for s in range(SLOTS):
        key = jnp.where(slot_of == s, (owner ^ FAR[1]) * rows, -rows)
        key = jnp.concatenate([key + r for r in range(rows)])
        pick.append((owner_row[:, None] == key[None, :]).astype(BF))
    update = pick_call(back.reshape(nf * rows, SLOTS * slab), jnp.stack(pick), rows).transpose(2, 0, 1)
    return (left_new[None], right_new[None], update)


def solution(mesh):
    nz = 32
    nf, nrep = mesh.shape["fsdp"], mesh.shape["rep"]
    mesh = Mesh(mesh.devices.reshape(nf // nz, nz, nrep // 2, 2), FSDP + REP)
    held = P(FSDP, None, REP, None)
    return jax.shard_map(
        on_device, mesh=mesh, in_specs=(P(REP, None, FSDP, None), P(), held, held, held, held),
        out_specs=(held, held, P(None, FSDP, REP)), check_vma=False)
```
